32 devices in a mesh: lat: 4 (over x, core), lev: 8 (over z, y).
Axes of the slice: x: 2, y: 2, z: 4, core: 2. Of those that a mesh axis runs over, the one named last changes fastest.
Arguments:
- spectral: float32 [2, 128, 256, 256], P(None, 'lev', 'lat'), may hold values from -6 to 6
- background: bfloat16 [384, 768, 128], P('lat', 'lev'), may hold values from -6 to 6
- columns: int32 [32, 2048], P(('lat', 'lev')), may hold values from 0 to 9215
- counts: int32 [32], P(('lat', 'lev')), may hold values from 1 to 2048, 32768 in all
- radiances: bfloat16 [32, 2048, 512], P(('lat', 'lev')), may hold values from -6 to 6
- used_pairs: int32 [32, 2048], P(('lat', 'lev')), may hold values from 1 to 256
- channel_weight: float32 [512], replicated, may hold values from 0.25 to 4
- weight_in: bfloat16 [128, 1024], replicated, may hold values from -0.5 to 0.5
- weight_mid: bfloat16 [1024, 1024], replicated, may hold values from -0.1875 to 0.1875
- weight_out: bfloat16 [1024, 512], replicated, may hold values from -0.1875 to 0.1875
Outputs:
- spectral_grad: float32 [2, 128, 256, 256], P(None, 'lev', 'lat')
- grid_grad: float32 [384, 768, 128], P('lat', 'lev')
The draws below stay inside these ranges and needn't reach their ends.
Inputs may be any that keep to these rules, and one draw needn't show every extreme that they name: Entry [o, s] is the column of owner o's slot s inside o's region of 96 x 96 columns, numbered latitude-major; slots at or past counts[o] are unused. The counts sum to 32768, and the largest is exactly 2048. Block [o, s] uses channels 0 to 2 x used_pairs[o, s] - 1.
All inputs are finite; a program needn't handle non-finite values. No bound on the sum of `counts` on one device may be relied on, other than what follows from the above.
Results may differ from the reference program's by a relative error of at most 0.008.
Values may be sent and summed in bfloat16 or wider, within the bound.
A program may use at most 128 MiB of HBM per device.

```python
import math
import jax
import jax.numpy as jnp
import numpy as np
from jax import lax

LEV = 128
M = 256
N = 256
NLAT = 384
NLON = 768
H1 = 1024
H2 = 1024
CHAN = 512
BLK_DEV = 1024
CAP = 2048
TOTAL = 32768
CLAT = 96
CLON = 96
N_LEV = 8
DEVICES = 32


def with_ends(array, rng, low, top_value):
    longest = array.shape.index(max(array.shape))
    spots = []
    for shift in (0, 1):
        where = [jax.random.randint(jax.random.fold_in(rng, axis), (), 0, length) for axis, length in enumerate(array.shape)]
        where[longest] = (where[longest] + shift) % array.shape[longest]
        spots.append(tuple(where))
    return array.at[spots[0]].set(low).at[spots[1]].set(top_value)


def shard_levels(rng, extent, shards, low, top_value):
    gain, own = 1.0, jax.random.fold_in(rng, 6)
    for axis_at, blocks in shards:
        steps = jnp.exp(jax.random.uniform(jax.random.fold_in(own, axis_at), (blocks,), jnp.float32, low / len(shards), top_value / len(shards)))
        gain = gain * jnp.repeat(steps, extent[axis_at] // blocks).reshape([-1 if axis == axis_at else 1 for axis in range(len(extent))])
    return gain


def split_up(count, total, bound, lean):
    portions = [(1 << 20) // math.isqrt(standing ** lean) + 1 for standing in range(2, count + 1)]
    rest, given = total - bound - (count - 1), [1] * (count - 1)
    while rest > 0:
        free = [i for i in range(count - 1) if given[i] < bound]
        pool, left = sum([portions[i] for i in free]), rest
        for i in free:
            addition = min(bound - given[i], max(1, left * portions[i] // pool), rest)
            given[i] = given[i] + addition
            rest = rest - addition
    return np.array([bound] + given)


def uneven(rng, count, total, reach, skew):
    if count == 2:
        one = jax.random.randint(rng, (), max(1, total - reach), min(reach, total - 1) + 1)
        return jnp.stack([one, total - one])
    tallies = jnp.asarray(split_up(count, total, reach, skew), jnp.int32)
    pairs = (count - 1) // 2
    source_of, sink = tallies[1:1 + 2 * pairs:2], tallies[2:2 + 2 * pairs:2]
    margin = jnp.minimum(source_of - 1, reach - sink)
    moved = jax.random.randint(jax.random.fold_in(rng, 1), (pairs,), 0, 1 << 20) % (margin + 1)
    tallies = tallies.at[1:1 + 2 * pairs:2].set(source_of - moved).at[2:2 + 2 * pairs:2].set(sink + moved)
    return tallies[jax.random.permutation(jax.random.fold_in(rng, 2), count)]


def scatter_about(rng, shape, deviation, reach, shards=(), held_as=jnp.bfloat16):
    values = deviation * jax.random.normal(rng, shape, jnp.float32)
    if shards:
        values = values * shard_levels(rng, shape, shards, -0.22, 0.18)
    return jnp.clip(values, -reach, reach).astype(held_as)


def setup_inputs(seed: int = 0) -> dict:
    keys = jax.random.split(jax.random.key(seed), 11)
    return {
        "spectral": scatter_about(keys[0], (2, LEV, M, N), 1.0, 6.0, ((1, 8), (2, 4)), jnp.float32),
        "background": scatter_about(keys[1], (NLAT, NLON, LEV), 1.0, 6.0, ((0, 4), (1, 8))),
        "columns": with_ends(jax.random.randint(keys[2], (DEVICES, CAP), 0, CLAT * CLON), jax.random.fold_in(keys[2], 1), 0, (CLAT * CLON) - 1).astype(jnp.int32),
        "counts": uneven(keys[3], DEVICES, TOTAL, CAP, 2).astype(jnp.int32),
        "radiances": scatter_about(keys[4], (DEVICES, CAP, CHAN), 1.0, 6.0, ((0, 32),)),
        "used_pairs": with_ends(jax.random.randint(keys[5], (DEVICES, CAP), 1, CHAN // 2 + 1), jax.random.fold_in(keys[5], 1), 1, (CHAN // 2 + 1) - 1).astype(jnp.int32),
        "channel_weight": jnp.clip(jnp.exp(jax.random.uniform(keys[6], (CHAN,), jnp.float32, math.log(0.25), math.log(4.0))), 0.25, 4.0),
        "weight_in": scatter_about(keys[7], (LEV, H1), LEV ** -0.5, 0.5),
        "weight_mid": scatter_about(keys[8], (H1, H2), H1 ** -0.5, 0.1875),
        "weight_out": scatter_about(keys[9], (H2, CHAN), H2 ** -0.5, 0.1875),
    }


RESCALE_TOP = 2.0 ** 60
RESCALE_BY = 2.0 ** (-60)
RESCALE_LOG = 60.0 * math.log(2.0)
HALF_LOG = 0.5 * math.log(0.5)

def legendre_table(orders, lat_total, degree_total):
    m_float = orders.astype(jnp.float32)
    lat_ids = jnp.arange(lat_total, dtype=jnp.float32)
    latitude = (0.5 - (lat_ids + 0.5) / lat_total) * jnp.pi
    sin_lat = jnp.sin(latitude)
    cos_lat = jnp.cos(latitude)
    order_ids = jnp.arange(1, degree_total, dtype=jnp.float32)
    log_steps = 0.5 * jnp.log((2.0 * order_ids + 1.0) / (2.0 * order_ids))
    log_norm = lax.optimization_barrier(jnp.sum(jnp.where(order_ids[None, :] <= m_float[:, None], log_steps[None, :], 0.0), axis=1))
    log_start = HALF_LOG + log_norm[:, None] + m_float[:, None] * jnp.log(cos_lat)[None, :]

    def advance(recur_state, degree):
        previous, earlier, shifts = recur_state
        n_float = degree.astype(jnp.float32)
        on_diagonal = (n_float == m_float)[:, None]
        next_diag = (n_float == m_float + 1.0)[:, None]
        beyond = (n_float > m_float + 1.0)[:, None]
        factor_a = jnp.sqrt(jnp.maximum(4.0 * n_float * n_float - 1.0, 1.0) / jnp.maximum(n_float * n_float - m_float * m_float, 1.0))
        lower = n_float - 1.0
        factor_b = jnp.sqrt(jnp.maximum(lower * lower - m_float * m_float, 0.0) / jnp.maximum(4.0 * lower * lower - 1.0, 1.0))
        current = jnp.where(beyond, factor_a[:, None] * (sin_lat[None, :] * previous - factor_b[:, None] * earlier), 0.0)
        current = jnp.where(next_diag, jnp.sqrt(2.0 * m_float + 3.0)[:, None] * sin_lat[None, :] * previous, current)
        current = jnp.where(on_diagonal, 1.0, current)
        oversized = jnp.abs(current) > RESCALE_TOP
        current = jnp.where(oversized, current * RESCALE_BY, current)
        previous = jnp.where(oversized, previous * RESCALE_BY, previous)
        shifts = shifts + oversized.astype(jnp.float32)
        values = current * jnp.exp(log_start + shifts * RESCALE_LOG)
        return ((current, previous, shifts), values)
    zeros = jnp.zeros((orders.shape[0], lat_total), jnp.float32)
    _, legendre = lax.scan(advance, (zeros, zeros, zeros), jnp.arange(degree_total, dtype=jnp.int32))
    return legendre

def wave_table(wave_total, lon_total):
    wave_ids = jnp.arange(wave_total, dtype=jnp.int32)
    lon_ids = jnp.arange(lon_total, dtype=jnp.int32)
    phase = (wave_ids[:, None] * lon_ids[None, :] % lon_total).astype(jnp.float32) * (2.0 * math.pi / lon_total)
    weights = jnp.where(wave_ids == 0, 1.0, 2.0).astype(jnp.float32) / wave_total
    return jnp.stack([weights[:, None] * jnp.cos(phase), -weights[:, None] * jnp.sin(phase)])

def silu_slope(inputs):
    sigmoid_v = jax.nn.sigmoid(inputs)
    return sigmoid_v * (1.0 + inputs * (1.0 - sigmoid_v))

def radiance_pass(profiles, observed, pair_counts, usable, channel_weight, weight_in, weight_mid, weight_out):
    pre_first = jnp.dot(profiles, weight_in, preferred_element_type=jnp.float32)
    act_first = jax.nn.silu(pre_first).astype(jnp.bfloat16)
    pre_second = jnp.dot(act_first, weight_mid, preferred_element_type=jnp.float32)
    act_second = jax.nn.silu(pre_second).astype(jnp.bfloat16)
    evolved = jnp.dot(act_second, weight_out, preferred_element_type=jnp.float32)
    channel_ids = jnp.arange(weight_out.shape[1], dtype=jnp.float32)
    active = (channel_ids[None, :] < 2.0 * pair_counts[:, None]) & usable[:, None]
    misfit = jnp.where(active, channel_weight[None, :] * (evolved - observed.astype(jnp.float32)), 0.0).astype(jnp.bfloat16)
    back_second = (jnp.dot(misfit, weight_out.T, preferred_element_type=jnp.float32) * silu_slope(pre_second)).astype(jnp.bfloat16)
    back_first = (jnp.dot(back_second, weight_mid.T, preferred_element_type=jnp.float32) * silu_slope(pre_first)).astype(jnp.bfloat16)
    return jnp.dot(back_first, weight_in.T, preferred_element_type=jnp.float32).astype(jnp.bfloat16)

def reference(spectral, background, columns, counts, radiances, used_pairs, channel_weight, weight_in, weight_mid, weight_out):
    highest = lax.Precision.HIGHEST
    legendre = legendre_table(jnp.arange(M, dtype=jnp.int32), NLAT, N)
    fourier = jnp.einsum('nmj,clmn->clmj', legendre, spectral, precision=highest)
    dft_table = wave_table(M, NLON)
    increment = jnp.einsum('clmj,cmx->jxl', fourier, dft_table, precision=highest)
    grid_state = (background.astype(jnp.float32) + increment).astype(jnp.bfloat16)
    start_ranks = (jnp.cumsum(counts) - counts).astype(jnp.int32)
    block_rank = jnp.arange(TOTAL, dtype=jnp.int32)
    covers = start_ranks[None, :] <= block_rank[:, None]
    owner_ids = (lax.optimization_barrier(jnp.sum(covers.astype(jnp.int32), axis=1)) - 1).astype(jnp.int32)
    slot_ids = (block_rank - start_ranks[owner_ids]).astype(jnp.int32)
    local_cols = columns[owner_ids, slot_ids]
    lat_ids = owner_ids // N_LEV * CLAT + local_cols // CLON
    lon_ids = owner_ids % N_LEV * CLON + local_cols % CLON
    flat_cells = (lat_ids * NLON + lon_ids).astype(jnp.int32)
    profiles = grid_state.reshape(NLAT * NLON, LEV)[flat_cells]
    observed = radiances[owner_ids, slot_ids]
    pair_counts = used_pairs[owner_ids, slot_ids].astype(jnp.float32)
    batches = TOTAL // BLK_DEV

    def one_batch(batch_rows):
        return radiance_pass(batch_rows[0], batch_rows[1], batch_rows[2], jnp.ones((BLK_DEV,), jnp.bool_), channel_weight, weight_in, weight_mid, weight_out)
    block_grad = lax.map(one_batch, (profiles.reshape(batches, BLK_DEV, LEV), observed.reshape(batches, BLK_DEV, CHAN), pair_counts.reshape(batches, BLK_DEV)))
    grid_grad = jnp.zeros((NLAT * NLON, LEV), jnp.float32).at[flat_cells].add(block_grad.reshape(TOTAL, LEV).astype(jnp.float32))
    grid_grad = grid_grad.reshape(NLAT, NLON, LEV)
    coeff_grad = jnp.einsum('jxl,cmx->clmj', grid_grad, dft_table, precision=highest)
    spectral_grad = jnp.einsum('nmj,clmj->clmn', legendre, coeff_grad, precision=highest)
    return (spectral_grad, grid_grad)
```

```python
import functools
import math

import jax
import jax.numpy as jnp
from jax import lax
from jax.experimental import pallas as pl
from jax.experimental.pallas import tpu as pltpu
from jax.sharding import PartitionSpec as P

M = 256
N = 256
NLAT = 384
NLON = 768


RESCALE_BY = 2.0 ** (-60)
RESCALE_LOG = 60.0 * math.log(2.0)
HALF_LOG = 0.5 * math.log(0.5)


CHUNK = 8
GROUP = 16
HALF = 128
SCALE_TOP = 2.0**20


def recurrence_inputs(orders, lat_total, degree_total):
    m_float = orders.astype(jnp.float32)
    half_lats = lat_total // 2
    lat_ids = jnp.arange(half_lats, dtype=jnp.float32)
    latitude = (0.5 - (lat_ids + 0.5) / lat_total) * jnp.pi
    order_ids = jnp.arange(1, degree_total, dtype=jnp.float32)
    log_steps = 0.5 * jnp.log((2.0 * order_ids + 1.0) / (2.0 * order_ids))
    log_norm = jnp.sum(
        jnp.where(order_ids[None, :] <= m_float[:, None], log_steps[None, :], 0.0), axis=1
    )
    log_cos = jnp.log(jnp.cos(latitude))
    log_start = HALF_LOG + log_norm[:, None] + m_float[:, None] * log_cos[None, :]
    pad = 2 * HALF - half_lats
    log_start = jnp.pad(log_start, ((0, 0), (0, pad)))
    sin_lat = jnp.pad(jnp.sin(latitude), (0, pad))[None, :]
    valid = jnp.pad(jnp.ones((half_lats,), jnp.float32), (0, pad))[None, :]
    n_float = jnp.arange(degree_total, dtype=jnp.float32)[None, :]
    m_col = m_float[:, None]
    factor_a = jnp.sqrt(
        jnp.maximum(4.0 * n_float * n_float - 1.0, 1.0)
        / jnp.maximum(n_float * n_float - m_col * m_col, 1.0)
    )
    lower = n_float - 1.0
    factor_b = jnp.sqrt(
        jnp.maximum(lower * lower - m_col * m_col, 0.0)
        / jnp.maximum(4.0 * lower * lower - 1.0, 1.0)
    )

    def chunks(factor):
        folded = factor.reshape(factor.shape[0], degree_total // CHUNK, CHUNK)
        return jnp.transpose(folded, (1, 0, 2))

    return chunks(factor_a), chunks(factor_a * factor_b), log_start, sin_lat, valid


def reversal(size, count):
    rows = lax.broadcasted_iota(jnp.int32, (size, size), 0)
    cols = lax.broadcasted_iota(jnp.int32, (size, size), 1)
    return jnp.where(rows + cols == count - 1, 1.0, 0.0).astype(jnp.bfloat16)


def synthesis_kernel(
    half_lats, fa_ref, fb_ref, log_ref, sin_ref, valid_ref, ord_ref, spec_ref,
    table_ref, four_ref, held
):
    steps = fa_ref.shape[0]
    degrees = steps * CHUNK
    lanes = 2 * HALF
    sin_lat = jnp.broadcast_to(sin_ref[...], (GROUP, lanes))
    valid = jnp.broadcast_to(valid_ref[...], (GROUP, lanes))
    order = ord_ref[...]
    log_start = log_ref[...]

    def step(chunk, state):
        previous, earlier, shifts = state
        scale = jnp.exp(log_start + shifts * RESCALE_LOG) * valid
        col_a = fa_ref[chunk]
        col_b = fb_ref[chunk]
        for k in range(CHUNK):
            degree = chunk * CHUNK + k
            current = (col_a[:, k : k + 1] * sin_lat) * previous - col_b[:, k : k + 1] * earlier
            current = jnp.where(order == degree, 1.0, current)
            values = current * scale
            at = pl.multiple_of(degree * GROUP, GROUP)
            held[0, pl.ds(at, GROUP), :] = values[:, :HALF]
            held[1, pl.ds(at, GROUP), :] = values[:, HALF:]
            earlier, previous = previous, current
        oversized = jnp.maximum(jnp.abs(previous), jnp.abs(earlier)) > SCALE_TOP
        factor = jnp.where(oversized, RESCALE_BY, 1.0)
        return previous * factor, earlier * factor, shifts + jnp.where(oversized, 1.0, 0.0)

    zeros = jnp.zeros((GROUP, lanes), jnp.float32)
    lax.fori_loop(0, steps, step, (zeros, zeros, zeros))

    bands = four_ref.shape[0]
    band = half_lats * 2 // bands
    flip = reversal(lanes, half_lats)
    parity = lax.broadcasted_iota(jnp.int32, spec_ref.shape[1:], 1) % 2
    count = spec_ref.shape[1]
    for m in range(GROUP):
        rows = pl.ds(m, degrees, stride=GROUP)
        table = jnp.concatenate(
            [held[0, rows, :].astype(jnp.bfloat16), held[1, rows, :].astype(jnp.bfloat16)], axis=1
        )
        table_ref[m] = table
        coeffs = spec_ref[m].astype(jnp.float32)
        even = jnp.where(parity == 0, coeffs, 0.0)
        both = jnp.concatenate([even, coeffs - even], axis=0).astype(jnp.bfloat16)
        sums = jnp.dot(both, table, preferred_element_type=jnp.float32)
        north = sums[:count] + sums[count:]
        south = sums[:count] - sums[count:]
        if m % 2:
            south = -south
        south = jnp.dot(south.astype(jnp.bfloat16), flip, preferred_element_type=jnp.float32)
        for b in range(bands // 2):
            four_ref[b, m] = north[:, b * band : (b + 1) * band].astype(jnp.bfloat16)
            four_ref[bands // 2 + b, m] = south[:, b * band : (b + 1) * band].astype(jnp.bfloat16)


def analysis_kernel(half_lats, coeff_ref, table_ref, out_ref):
    bands, group, count, band = coeff_ref.shape
    lanes = 2 * HALF
    flip = reversal(lanes, half_lats)
    parity = lax.broadcasted_iota(jnp.int32, out_ref.shape[1:], 1) % 2
    fill = jnp.zeros((count, lanes - half_lats), jnp.float32)
    for m in range(group):
        bits = [coeff_ref[b, m].astype(jnp.float32) for b in range(bands)]
        north = jnp.concatenate(bits[: bands // 2] + [fill], axis=1)
        south = jnp.concatenate(bits[bands // 2 :] + [fill], axis=1).astype(jnp.bfloat16)
        south = jnp.dot(south, flip, preferred_element_type=jnp.float32)
        if m % 2:
            south = -south
        both = jnp.concatenate([north + south, north - south], axis=0).astype(jnp.bfloat16)
        sums = lax.dot_general(
            both, table_ref[m], (((1,), (1,)), ((), ())), preferred_element_type=jnp.float32
        )
        out_ref[m] = jnp.where(parity == 0, sums[:count], sums[count:])


def synthesis(spectral, orders, lat_total, bands):
    parts, levels, waves, degrees = spectral.shape
    half_lats = lat_total // 2
    count = parts * levels
    lanes = 2 * HALF
    fa, fb, log_start, sin_lat, valid = recurrence_inputs(orders, lat_total, degrees)
    order = jnp.broadcast_to(orders[:, None], (waves, lanes))
    coeffs = jnp.transpose(spectral.astype(jnp.bfloat16), (2, 0, 1, 3)).reshape(
        waves, count, degrees
    )
    band = lat_total // bands
    factor_spec = pl.BlockSpec((degrees // CHUNK, GROUP, CHUNK), lambda g: (0, g, 0))
    wide_spec = pl.BlockSpec((GROUP, lanes), lambda g: (g, 0))
    row_spec = pl.BlockSpec((1, lanes), lambda g: (0, 0))
    return pl.pallas_call(
        functools.partial(synthesis_kernel, half_lats),
        grid=(waves // GROUP,),
        in_specs=[
            factor_spec,
            factor_spec,
            wide_spec,
            row_spec,
            row_spec,
            wide_spec,
            pl.BlockSpec((GROUP, count, degrees), lambda g: (g, 0, 0)),
        ],
        out_specs=[
            pl.BlockSpec((GROUP, degrees, lanes), lambda g: (g, 0, 0)),
            pl.BlockSpec((bands, GROUP, count, band), lambda g: (0, g, 0, 0)),
        ],
        out_shape=[
            jax.ShapeDtypeStruct((waves, degrees, lanes), jnp.bfloat16),
            jax.ShapeDtypeStruct((bands, waves, count, band), jnp.bfloat16),
        ],
        scratch_shapes=[pltpu.VMEM((2, degrees * GROUP, HALF), jnp.float32)],
        compiler_params=pltpu.CompilerParams(vmem_limit_bytes=40 << 20),
    )(fa, fb, log_start, sin_lat, valid, order, coeffs)


def analysis(coeffs, table, lat_total):
    bands, waves, count, band = coeffs.shape
    degrees, lanes = table.shape[1:]
    group = 8
    return pl.pallas_call(
        functools.partial(analysis_kernel, lat_total // 2),
        grid=(waves // group,),
        in_specs=[
            pl.BlockSpec((bands, group, count, band), lambda g: (0, g, 0, 0)),
            pl.BlockSpec((group, degrees, lanes), lambda g: (g, 0, 0)),
        ],
        out_specs=pl.BlockSpec((group, count, degrees), lambda g: (g, 0, 0)),
        out_shape=jax.ShapeDtypeStruct((waves, count, degrees), jnp.float32),
        compiler_params=pltpu.CompilerParams(vmem_limit_bytes=40 << 20),
    )(coeffs, table)


def wave_table(wave_total, lon_total):
    wave_ids = jnp.arange(wave_total, dtype=jnp.int32)
    lon_ids = jnp.arange(lon_total, dtype=jnp.int32)
    phase = (wave_ids[:, None] * lon_ids[None, :] % lon_total).astype(jnp.float32) * (
        2.0 * math.pi / lon_total
    )
    weights = jnp.where(wave_ids == 0, 1.0, 2.0).astype(jnp.float32) / wave_total
    return jnp.stack([weights[:, None] * jnp.cos(phase), -weights[:, None] * jnp.sin(phase)])


def silu_slope(inputs):
    sigmoid_v = jax.nn.sigmoid(inputs)
    return sigmoid_v * (1.0 + inputs * (1.0 - sigmoid_v))


def radiance_pass(
    profiles, observed, pair_counts, usable, channel_weight, weight_in, weight_mid, weight_out
):
    pre_first = jnp.dot(profiles, weight_in, preferred_element_type=jnp.float32)
    act_first = jax.nn.silu(pre_first).astype(jnp.bfloat16)
    pre_second = jnp.dot(act_first, weight_mid, preferred_element_type=jnp.float32)
    act_second = jax.nn.silu(pre_second).astype(jnp.bfloat16)
    evolved = jnp.dot(act_second, weight_out, preferred_element_type=jnp.float32)
    channel_ids = jnp.arange(weight_out.shape[1], dtype=jnp.float32)
    active = (channel_ids[None, :] < 2.0 * pair_counts[:, None]) & usable[:, None]
    misfit = jnp.where(
        active, channel_weight[None, :] * (evolved - observed.astype(jnp.float32)), 0.0
    ).astype(jnp.bfloat16)
    back_second = (
        jnp.dot(misfit, weight_out.T, preferred_element_type=jnp.float32) * silu_slope(pre_second)
    ).astype(jnp.bfloat16)
    back_first = (
        jnp.dot(back_second, weight_mid.T, preferred_element_type=jnp.float32)
        * silu_slope(pre_first)
    ).astype(jnp.bfloat16)
    return jnp.dot(back_first, weight_in.T, preferred_element_type=jnp.float32).astype(jnp.bfloat16)


def per_device(
    spectral,
    background,
    columns,
    counts,
    radiances,
    used_pairs,
    channel_weight,
    weight_in,
    weight_mid,
    weight_out,
):
    lat_index = lax.axis_index("lat")
    parts, levels, waves_local, degrees = spectral.shape
    bands = M // waves_local
    orders = lat_index * waves_local + jnp.arange(waves_local, dtype=jnp.int32)
    table, fourier = synthesis(spectral, orders, NLAT, bands)
    fourier = lax.all_to_all(fourier, "lat", split_axis=0, concat_axis=0, tiled=True)
    band = fourier.shape[3]
    fourier = fourier.reshape(M, parts, levels, band)
    dft_table = wave_table(M, NLON).astype(jnp.bfloat16)
    increment = jnp.einsum(
        "mclj,cmx->jlx", fourier, dft_table, preferred_element_type=jnp.float32
    ).astype(jnp.bfloat16)
    increment = lax.all_to_all(increment, "lev", split_axis=2, concat_axis=1, tiled=True)
    increment = jnp.transpose(increment, (0, 2, 1)).astype(jnp.float32)
    grid_state = (background.astype(jnp.float32) + increment).astype(jnp.bfloat16)
    band_rows = grid_state.shape[0]
    tile_cols = grid_state.shape[1]
    cell_rows = grid_state.reshape(band_rows * tile_cols, grid_state.shape[2])
    local_cols = columns[0]
    profiles = jnp.take(cell_rows, local_cols, axis=0)
    capacity = local_cols.shape[0]
    usable = jnp.arange(capacity, dtype=jnp.int32) < counts[0]
    observed = radiances[0]
    pair_counts = used_pairs[0].astype(jnp.float32)
    block_grad = radiance_pass(
        profiles, observed, pair_counts, usable, channel_weight, weight_in, weight_mid, weight_out
    )
    grid_grad = (
        jnp.zeros(cell_rows.shape, jnp.float32).at[local_cols].add(block_grad.astype(jnp.float32))
    )
    grid_grad = grid_grad.reshape(band_rows, tile_cols, cell_rows.shape[1])
    grad_rows = lax.all_to_all(
        jnp.transpose(grid_grad, (0, 2, 1)).astype(jnp.bfloat16),
        "lev",
        split_axis=1,
        concat_axis=2,
        tiled=True,
    )
    coeff_grad = jnp.einsum(
        "jlx,cmx->mclj", grad_rows, dft_table, preferred_element_type=jnp.float32
    ).astype(jnp.bfloat16)
    coeff_grad = coeff_grad.reshape(bands, waves_local, parts * levels, band)
    coeff_grad = lax.all_to_all(coeff_grad, "lat", split_axis=0, concat_axis=0, tiled=True)
    spectral_grad = analysis(coeff_grad, table, NLAT)
    spectral_grad = jnp.transpose(
        spectral_grad.reshape(waves_local, parts, levels, degrees), (1, 2, 0, 3)
    )
    return (spectral_grad, grid_grad)


def solution(mesh):
    in_specs = (
        P(None, "lev", "lat", None),
        P("lat", "lev", None),
        P(("lat", "lev"), None),
        P(("lat", "lev")),
        P(("lat", "lev"), None, None),
        P(("lat", "lev"), None),
        P(),
        P(),
        P(),
        P(),
    )
    out_specs = (P(None, "lev", "lat", None), P("lat", "lev", None))
    return jax.shard_map(
        per_device, mesh=mesh, in_specs=in_specs, out_specs=out_specs, check_vma=False
    )
```

```python
import functools
import math

import jax
import jax.numpy as jnp
from jax import lax
from jax.experimental import pallas as pl
from jax.experimental.pallas import tpu as pltpu
from jax.sharding import PartitionSpec as P

M = 256
N = 256
NLAT = 384
NLON = 768


RESCALE_BY = 2.0 ** (-60)
RESCALE_LOG = 60.0 * math.log(2.0)
HALF_LOG = 0.5 * math.log(0.5)


CHUNK = 8
GROUP = 16
HALF = 128
SCALE_TOP = 2.0**20


def recurrence_inputs(orders, lat_total, degree_total):
    m_float = orders.astype(jnp.float32)
    half_lats = lat_total // 2
    lat_ids = jnp.arange(half_lats, dtype=jnp.float32)
    latitude = (0.5 - (lat_ids + 0.5) / lat_total) * jnp.pi
    order_ids = jnp.arange(1, degree_total, dtype=jnp.float32)
    log_steps = 0.5 * jnp.log((2.0 * order_ids + 1.0) / (2.0 * order_ids))
    log_norm = jnp.sum(
        jnp.where(order_ids[None, :] <= m_float[:, None], log_steps[None, :], 0.0), axis=1
    )
    log_cos = jnp.log(jnp.cos(latitude))
    log_start = HALF_LOG + log_norm[:, None] + m_float[:, None] * log_cos[None, :]
    pad = 2 * HALF - half_lats
    log_start = jnp.pad(log_start, ((0, 0), (0, pad)))
    sin_lat = jnp.pad(jnp.sin(latitude), (0, pad))[None, :]
    valid = jnp.pad(jnp.ones((half_lats,), jnp.float32), (0, pad))[None, :]
    n_float = jnp.arange(degree_total, dtype=jnp.float32)[None, :]
    m_col = m_float[:, None]
    factor_a = jnp.sqrt(
        jnp.maximum(4.0 * n_float * n_float - 1.0, 1.0)
        / jnp.maximum(n_float * n_float - m_col * m_col, 1.0)
    )
    lower = n_float - 1.0
    factor_b = jnp.sqrt(
        jnp.maximum(lower * lower - m_col * m_col, 0.0)
        / jnp.maximum(4.0 * lower * lower - 1.0, 1.0)
    )

    def chunks(factor):
        folded = factor.reshape(factor.shape[0], degree_total // CHUNK, CHUNK)
        return jnp.transpose(folded, (1, 0, 2))

    return chunks(factor_a), chunks(factor_a * factor_b), log_start, sin_lat, valid


def reversal(size, count):
    rows = lax.broadcasted_iota(jnp.int32, (size, size), 0)
    cols = lax.broadcasted_iota(jnp.int32, (size, size), 1)
    return jnp.where(rows + cols == count - 1, 1.0, 0.0).astype(jnp.bfloat16)


def synthesis_kernel(
    half_lats, fa_ref, fb_ref, log_ref, sin_ref, valid_ref, ord_ref, spec_ref,
    table_ref, four_ref, held
):
    steps = fa_ref.shape[0]
    degrees = steps * CHUNK
    lanes = 2 * HALF
    sin_lat = jnp.broadcast_to(sin_ref[...], (GROUP, lanes))
    valid = jnp.broadcast_to(valid_ref[...], (GROUP, lanes))
    order = ord_ref[...]
    log_start = log_ref[...]

    def step(chunk, state):
        previous, earlier, shifts = state
        scale = jnp.exp(log_start + shifts * RESCALE_LOG) * valid
        col_a = fa_ref[chunk]
        col_b = fb_ref[chunk]
        for k in range(CHUNK):
            degree = chunk * CHUNK + k
            current = (col_a[:, k : k + 1] * sin_lat) * previous - col_b[:, k : k + 1] * earlier
            current = jnp.where(order == degree, 1.0, current)
            values = current * scale
            at = pl.multiple_of(degree * GROUP, GROUP)
            held[0, pl.ds(at, GROUP), :] = values[:, :HALF]
            held[1, pl.ds(at, GROUP), :] = values[:, HALF:]
            earlier, previous = previous, current
        oversized = jnp.maximum(jnp.abs(previous), jnp.abs(earlier)) > SCALE_TOP
        factor = jnp.where(oversized, RESCALE_BY, 1.0)
        return previous * factor, earlier * factor, shifts + jnp.where(oversized, 1.0, 0.0)

    zeros = jnp.zeros((GROUP, lanes), jnp.float32)
    lax.fori_loop(0, steps, step, (zeros, zeros, zeros))

    bands = four_ref.shape[0]
    band = half_lats * 2 // bands
    flip = reversal(lanes, half_lats)
    parity = lax.broadcasted_iota(jnp.int32, spec_ref.shape[1:], 1) % 2
    count = spec_ref.shape[1]
    for m in range(GROUP):
        rows = pl.ds(m, degrees, stride=GROUP)
        table = jnp.concatenate(
            [held[0, rows, :].astype(jnp.bfloat16), held[1, rows, :].astype(jnp.bfloat16)], axis=1
        )
        table_ref[m] = table
        coeffs = spec_ref[m].astype(jnp.float32)
        even = jnp.where(parity == 0, coeffs, 0.0)
        both = jnp.concatenate([even, coeffs - even], axis=0).astype(jnp.bfloat16)
        sums = jnp.dot(both, table, preferred_element_type=jnp.float32)
        north = sums[:count] + sums[count:]
        south = sums[:count] - sums[count:]
        if m % 2:
            south = -south
        south = jnp.dot(south.astype(jnp.bfloat16), flip, preferred_element_type=jnp.float32)
        for b in range(bands // 2):
            four_ref[b, m] = north[:, b * band : (b + 1) * band].astype(jnp.bfloat16)
            four_ref[bands // 2 + b, m] = south[:, b * band : (b + 1) * band].astype(jnp.bfloat16)


def analysis_kernel(half_lats, coeff_ref, table_ref, out_ref):
    bands, group, count, band = coeff_ref.shape
    lanes = 2 * HALF
    flip = reversal(lanes, half_lats)
    parity = lax.broadcasted_iota(jnp.int32, out_ref.shape[1:], 1) % 2
    fill = jnp.zeros((count, lanes - half_lats), jnp.float32)
    for m in range(group):
        bits = [coeff_ref[b, m].astype(jnp.float32) for b in range(bands)]
        north = jnp.concatenate(bits[: bands // 2] + [fill], axis=1)
        south = jnp.concatenate(bits[bands // 2 :] + [fill], axis=1).astype(jnp.bfloat16)
        south = jnp.dot(south, flip, preferred_element_type=jnp.float32)
        if m % 2:
            south = -south
        both = jnp.concatenate([north + south, north - south], axis=0).astype(jnp.bfloat16)
        sums = lax.dot_general(
            both, table_ref[m], (((1,), (1,)), ((), ())), preferred_element_type=jnp.float32
        )
        out_ref[m] = jnp.where(parity == 0, sums[:count], sums[count:])


def synthesis(spectral, orders, lat_total, bands):
    parts, levels, waves, degrees = spectral.shape
    half_lats = lat_total // 2
    count = parts * levels
    lanes = 2 * HALF
    fa, fb, log_start, sin_lat, valid = recurrence_inputs(orders, lat_total, degrees)
    order = jnp.broadcast_to(orders[:, None], (waves, lanes))
    coeffs = jnp.transpose(spectral.astype(jnp.bfloat16), (2, 0, 1, 3)).reshape(
        waves, count, degrees
    )
    band = lat_total // bands
    factor_spec = pl.BlockSpec((degrees // CHUNK, GROUP, CHUNK), lambda g: (0, g, 0))
    wide_spec = pl.BlockSpec((GROUP, lanes), lambda g: (g, 0))
    row_spec = pl.BlockSpec((1, lanes), lambda g: (0, 0))
    return pl.pallas_call(
        functools.partial(synthesis_kernel, half_lats),
        grid=(waves // GROUP,),
        in_specs=[
            factor_spec,
            factor_spec,
            wide_spec,
            row_spec,
            row_spec,
            wide_spec,
            pl.BlockSpec((GROUP, count, degrees), lambda g: (g, 0, 0)),
        ],
        out_specs=[
            pl.BlockSpec((GROUP, degrees, lanes), lambda g: (g, 0, 0)),
            pl.BlockSpec((bands, GROUP, count, band), lambda g: (0, g, 0, 0)),
        ],
        out_shape=[
            jax.ShapeDtypeStruct((waves, degrees, lanes), jnp.bfloat16),
            jax.ShapeDtypeStruct((bands, waves, count, band), jnp.bfloat16),
        ],
        scratch_shapes=[pltpu.VMEM((2, degrees * GROUP, HALF), jnp.float32)],
        compiler_params=pltpu.CompilerParams(vmem_limit_bytes=40 << 20),
    )(fa, fb, log_start, sin_lat, valid, order, coeffs)


def analysis(coeffs, table, lat_total):
    bands, waves, count, band = coeffs.shape
    degrees, lanes = table.shape[1:]
    group = 8
    return pl.pallas_call(
        functools.partial(analysis_kernel, lat_total // 2),
        grid=(waves // group,),
        in_specs=[
            pl.BlockSpec((bands, group, count, band), lambda g: (0, g, 0, 0)),
            pl.BlockSpec((group, degrees, lanes), lambda g: (g, 0, 0)),
        ],
        out_specs=pl.BlockSpec((group, count, degrees), lambda g: (g, 0, 0)),
        out_shape=jax.ShapeDtypeStruct((waves, count, degrees), jnp.float32),
        compiler_params=pltpu.CompilerParams(vmem_limit_bytes=40 << 20),
    )(coeffs, table)


def pick_kernel(index_ref, shift_ref, count_ref, grid_ref, out_ref):
    target = pl.program_id(0)
    levels, capacity = out_ref.shape[1:]
    out_ref[...] = jnp.zeros(out_ref.shape, out_ref.dtype)
    lane = lax.broadcasted_iota(jnp.int32, (levels, HALF), 1)

    def block(b, carry):
        base = b * HALF
        total = jnp.zeros((levels, HALF), jnp.float32)
        for q in range(HALF):
            at = target * capacity + base + q
            moved = pltpu.roll(grid_ref[index_ref[at]], shift_ref[at], 1)
            total = jnp.where(lane == q, moved, total)
        out_ref[0, :, pl.ds(pl.multiple_of(base, HALF), HALF)] = total.astype(out_ref.dtype)
        return carry

    lax.fori_loop(0, (count_ref[target] + HALF - 1) // HALF, block, 0)


def pick(index, shift, counts, grid, capacity):
    owners = counts.shape[0]
    levels = grid.shape[1]
    return pl.pallas_call(
        pick_kernel,
        grid_spec=pltpu.PrefetchScalarGridSpec(
            num_scalar_prefetch=3,
            grid=(owners,),
            in_specs=[pl.BlockSpec(grid.shape, lambda t, *_: (0, 0, 0))],
            out_specs=pl.BlockSpec((1, levels, capacity), lambda t, *_: (t, 0, 0)),
        ),
        out_shape=jax.ShapeDtypeStruct((owners, levels, capacity), jnp.bfloat16),
        compiler_params=pltpu.CompilerParams(vmem_limit_bytes=32 << 20),
    )(index, shift, counts, grid)


def spread_kernel(row_ref, lane_ref, count_ref, values_ref, out_ref, *sums):
    owners, levels, capacity = values_ref.shape
    lane = lax.broadcasted_iota(jnp.int32, (levels, HALF), 1)
    most = count_ref[0]
    for o in range(owners):
        sums[o][...] = jnp.zeros(sums[o].shape, jnp.float32)
        most = jnp.maximum(most, count_ref[o])

    def one(slot, carry):
        base = pl.multiple_of((slot // HALF) * HALF, HALF)
        spot = slot % HALF
        for o in range(owners):
            row = row_ref[o * capacity + slot]
            to = lane_ref[o * capacity + slot]
            values = values_ref[o, :, pl.ds(base, HALF)]
            moved = pltpu.roll(values, (to - spot + HALF) % HALF, 1)
            sums[o][row] = sums[o][row] + jnp.where(lane == to, moved, 0.0)
        return carry

    def several(group, carry):
        for k in range(4):
            one(group * 4 + k, carry)
        return carry

    lax.fori_loop(0, (most + 3) // 4, several, 0)
    for o in range(owners):
        out_ref[o] = sums[o][...].astype(out_ref.dtype)


def spread(rows, lanes, counts, values, band_rows):
    owners, levels, capacity = values.shape
    shape = (owners, band_rows, levels, HALF)
    return pl.pallas_call(
        spread_kernel,
        grid_spec=pltpu.PrefetchScalarGridSpec(
            num_scalar_prefetch=3,
            grid=(1,),
            in_specs=[pl.BlockSpec(values.shape, lambda g, *_: (0, 0, 0))],
            out_specs=pl.BlockSpec(shape, lambda g, *_: (0, 0, 0, 0)),
            scratch_shapes=[pltpu.VMEM(shape[1:], jnp.float32) for _ in range(owners)],
        ),
        out_shape=jax.ShapeDtypeStruct(shape, jnp.bfloat16),
        compiler_params=pltpu.CompilerParams(vmem_limit_bytes=40 << 20),
    )(rows, lanes, counts, values)


def wave_table(wave_total, lon_total):
    wave_ids = jnp.arange(wave_total, dtype=jnp.int32)
    lon_ids = jnp.arange(lon_total, dtype=jnp.int32)
    phase = (wave_ids[:, None] * lon_ids[None, :] % lon_total).astype(jnp.float32) * (
        2.0 * math.pi / lon_total
    )
    weights = jnp.where(wave_ids == 0, 1.0, 2.0).astype(jnp.float32) / wave_total
    return jnp.stack([weights[:, None] * jnp.cos(phase), -weights[:, None] * jnp.sin(phase)])


def silu_slope(inputs):
    sigmoid_v = jax.nn.sigmoid(inputs)
    return sigmoid_v * (1.0 + inputs * (1.0 - sigmoid_v))


def radiance_pass(
    profiles, observed, pair_counts, usable, channel_weight, weight_in, weight_mid, weight_out
):
    pre_first = jnp.dot(profiles, weight_in, preferred_element_type=jnp.float32)
    act_first = jax.nn.silu(pre_first).astype(jnp.bfloat16)
    pre_second = jnp.dot(act_first, weight_mid, preferred_element_type=jnp.float32)
    act_second = jax.nn.silu(pre_second).astype(jnp.bfloat16)
    evolved = jnp.dot(act_second, weight_out, preferred_element_type=jnp.float32)
    channel_ids = jnp.arange(weight_out.shape[1], dtype=jnp.float32)
    active = (channel_ids[None, :] < 2.0 * pair_counts[:, None]) & usable[:, None]
    misfit = jnp.where(
        active, channel_weight[None, :] * (evolved - observed.astype(jnp.float32)), 0.0
    ).astype(jnp.bfloat16)
    back_second = (
        jnp.dot(misfit, weight_out.T, preferred_element_type=jnp.float32) * silu_slope(pre_second)
    ).astype(jnp.bfloat16)
    back_first = (
        jnp.dot(back_second, weight_mid.T, preferred_element_type=jnp.float32)
        * silu_slope(pre_first)
    ).astype(jnp.bfloat16)
    return jnp.dot(back_first, weight_in.T, preferred_element_type=jnp.float32).astype(jnp.bfloat16)


def per_device(
    spectral,
    background,
    columns,
    counts,
    radiances,
    used_pairs,
    channel_weight,
    weight_in,
    weight_mid,
    weight_out,
):
    lat_index = lax.axis_index("lat")
    parts, levels, waves_local, degrees = spectral.shape
    bands = M // waves_local
    orders = lat_index * waves_local + jnp.arange(waves_local, dtype=jnp.int32)
    table, fourier = synthesis(spectral, orders, NLAT, bands)
    fourier = lax.all_to_all(fourier, "lat", split_axis=0, concat_axis=0, tiled=True)
    band = fourier.shape[3]
    fourier = fourier.reshape(M, parts, levels, band)
    dft_table = wave_table(M, NLON).astype(jnp.bfloat16)
    band_rows, tile_cols, all_levels = background.shape
    local_cols = columns[0]
    owners = all_levels // levels
    capacity = local_cols.shape[0]
    listed = lax.all_gather(local_cols, "lev")
    band_counts = lax.all_gather(counts, "lev", tiled=True)
    tiles = NLON // HALF
    list_rows = listed // tile_cols
    list_lanes = listed % tile_cols
    list_lons = list_lanes + jnp.arange(owners, dtype=jnp.int32)[:, None] * tile_cols
    spots = jnp.arange(capacity, dtype=jnp.int32) % HALF
    index = (list_rows * tiles + list_lons // HALF).reshape(-1)
    shift = ((spots[None, :] - list_lons) % HALF).reshape(-1)
    increment = jnp.einsum(
        "mclj,cmtx->jtlx",
        fourier,
        dft_table.reshape(parts, M, tiles, HALF),
        preferred_element_type=jnp.float32,
    ).reshape(band * tiles, levels, HALF)
    picked = pick(index, shift, band_counts, increment, capacity)
    picked = lax.all_to_all(picked, "lev", split_axis=0, concat_axis=0, tiled=True)
    picked = picked.reshape(all_levels, capacity)
    cell_rows = background.reshape(band_rows * tile_cols, all_levels)
    own_rows = jnp.take(cell_rows, local_cols, axis=0).astype(jnp.float32)
    profiles = (own_rows + picked.T.astype(jnp.float32)).astype(jnp.bfloat16)
    usable = jnp.arange(capacity, dtype=jnp.int32) < counts[0]
    observed = radiances[0]
    pair_counts = used_pairs[0].astype(jnp.float32)
    block_grad = radiance_pass(
        profiles, observed, pair_counts, usable, channel_weight, weight_in, weight_mid, weight_out
    )
    grid_grad = (
        jnp.zeros(cell_rows.shape, jnp.float32).at[local_cols].add(block_grad.astype(jnp.float32))
    )
    grid_grad = grid_grad.reshape(band_rows, tile_cols, all_levels)
    sent = block_grad.T.reshape(owners, levels, capacity)
    sent = lax.all_to_all(sent, "lev", split_axis=0, concat_axis=0, tiled=True)
    grad_rows = spread(
        list_rows.reshape(-1),
        list_lanes.reshape(-1),
        band_counts,
        sent.astype(jnp.float32),
        band_rows,
    )
    tile_table = dft_table.reshape(parts, M, owners, tile_cols)
    tile_table = jnp.pad(tile_table, ((0, 0), (0, 0), (0, 0), (0, HALF - tile_cols)))
    coeff_grad = jnp.einsum(
        "ojlx,cmox->mclj", grad_rows, tile_table, preferred_element_type=jnp.float32
    ).astype(jnp.bfloat16)
    coeff_grad = coeff_grad.reshape(bands, waves_local, parts * levels, band)
    coeff_grad = lax.all_to_all(coeff_grad, "lat", split_axis=0, concat_axis=0, tiled=True)
    spectral_grad = analysis(coeff_grad, table, NLAT)
    spectral_grad = jnp.transpose(
        spectral_grad.reshape(waves_local, parts, levels, degrees), (1, 2, 0, 3)
    )
    return (spectral_grad, grid_grad)


def solution(mesh):
    in_specs = (
        P(None, "lev", "lat", None),
        P("lat", "lev", None),
        P(("lat", "lev"), None),
        P(("lat", "lev")),
        P(("lat", "lev"), None, None),
        P(("lat", "lev"), None),
        P(),
        P(),
        P(),
        P(),
    )
    out_specs = (P(None, "lev", "lat", None), P("lat", "lev", None))
    return jax.shard_map(
        per_device, mesh=mesh, in_specs=in_specs, out_specs=out_specs, check_vma=False
    )
```

```python
import functools
import math

import jax
import jax.numpy as jnp
from jax import lax
from jax.experimental import pallas as pl
from jax.experimental.pallas import tpu as pltpu
from jax.sharding import PartitionSpec as P

M = 256
N = 256
NLAT = 384
NLON = 768


RESCALE_BY = 2.0 ** (-60)
RESCALE_LOG = 60.0 * math.log(2.0)
HALF_LOG = 0.5 * math.log(0.5)


CHUNK = 8
GROUP = 16
HALF = 128
SCALE_TOP = 2.0**20


def recurrence_inputs(orders, lat_total, degree_total):
    m_float = orders.astype(jnp.float32)
    half_lats = lat_total // 2
    lat_ids = jnp.arange(half_lats, dtype=jnp.float32)
    latitude = (0.5 - (lat_ids + 0.5) / lat_total) * jnp.pi
    order_ids = jnp.arange(1, degree_total, dtype=jnp.float32)
    log_steps = 0.5 * jnp.log((2.0 * order_ids + 1.0) / (2.0 * order_ids))
    log_norm = jnp.sum(
        jnp.where(order_ids[None, :] <= m_float[:, None], log_steps[None, :], 0.0), axis=1
    )
    log_cos = jnp.log(jnp.cos(latitude))
    log_start = HALF_LOG + log_norm[:, None] + m_float[:, None] * log_cos[None, :]
    pad = 2 * HALF - half_lats
    log_start = jnp.pad(log_start, ((0, 0), (0, pad)))
    sin_lat = jnp.pad(jnp.sin(latitude), (0, pad))[None, :]
    valid = jnp.pad(jnp.ones((half_lats,), jnp.float32), (0, pad))[None, :]
    n_float = jnp.arange(degree_total, dtype=jnp.float32)[None, :]
    m_col = m_float[:, None]
    factor_a = jnp.sqrt(
        jnp.maximum(4.0 * n_float * n_float - 1.0, 1.0)
        / jnp.maximum(n_float * n_float - m_col * m_col, 1.0)
    )
    lower = n_float - 1.0
    factor_b = jnp.sqrt(
        jnp.maximum(lower * lower - m_col * m_col, 0.0)
        / jnp.maximum(4.0 * lower * lower - 1.0, 1.0)
    )

    def chunks(factor):
        folded = factor.reshape(factor.shape[0], degree_total // CHUNK, CHUNK)
        return jnp.transpose(folded, (1, 0, 2))

    return chunks(factor_a), chunks(factor_a * factor_b), log_start, sin_lat, valid


def reversal(size, count):
    rows = lax.broadcasted_iota(jnp.int32, (size, size), 0)
    cols = lax.broadcasted_iota(jnp.int32, (size, size), 1)
    return jnp.where(rows + cols == count - 1, 1.0, 0.0).astype(jnp.bfloat16)


def synthesis_kernel(
    half_lats, fa_ref, fb_ref, log_ref, sin_ref, valid_ref, ord_ref, spec_ref,
    table_ref, four_ref, held
):
    steps = fa_ref.shape[0]
    degrees = steps * CHUNK
    lanes = 2 * HALF
    sin_lat = jnp.broadcast_to(sin_ref[...], (GROUP, lanes))
    valid = jnp.broadcast_to(valid_ref[...], (GROUP, lanes))
    order = ord_ref[...]
    log_start = log_ref[...]

    def step(chunk, state):
        previous, earlier, shifts = state
        scale = jnp.exp(log_start + shifts * RESCALE_LOG) * valid
        col_a = fa_ref[chunk]
        col_b = fb_ref[chunk]
        for k in range(CHUNK):
            degree = chunk * CHUNK + k
            current = (col_a[:, k : k + 1] * sin_lat) * previous - col_b[:, k : k + 1] * earlier
            current = jnp.where(order == degree, 1.0, current)
            values = current * scale
            at = pl.multiple_of(degree * GROUP, GROUP)
            held[0, pl.ds(at, GROUP), :] = values[:, :HALF]
            held[1, pl.ds(at, GROUP), :] = values[:, HALF:]
            earlier, previous = previous, current
        oversized = jnp.maximum(jnp.abs(previous), jnp.abs(earlier)) > SCALE_TOP
        factor = jnp.where(oversized, RESCALE_BY, 1.0)
        return previous * factor, earlier * factor, shifts + jnp.where(oversized, 1.0, 0.0)

    zeros = jnp.zeros((GROUP, lanes), jnp.float32)
    lax.fori_loop(0, steps, step, (zeros, zeros, zeros))

    bands = four_ref.shape[0]
    band = half_lats * 2 // bands
    flip = reversal(lanes, half_lats)
    parity = lax.broadcasted_iota(jnp.int32, spec_ref.shape[1:], 1) % 2
    count = spec_ref.shape[1]
    for m in range(GROUP):
        rows = pl.ds(m, degrees, stride=GROUP)
        table = jnp.concatenate(
            [held[0, rows, :].astype(jnp.bfloat16), held[1, rows, :].astype(jnp.bfloat16)], axis=1
        )
        table_ref[m] = table
        coeffs = spec_ref[m].astype(jnp.float32)
        even = jnp.where(parity == 0, coeffs, 0.0)
        both = jnp.concatenate([even, coeffs - even], axis=0).astype(jnp.bfloat16)
        sums = jnp.dot(both, table, preferred_element_type=jnp.float32)
        north = sums[:count] + sums[count:]
        south = sums[:count] - sums[count:]
        if m % 2:
            south = -south
        south = jnp.dot(south.astype(jnp.bfloat16), flip, preferred_element_type=jnp.float32)
        for b in range(bands // 2):
            four_ref[b, m] = north[:, b * band : (b + 1) * band].astype(jnp.bfloat16)
            four_ref[bands // 2 + b, m] = south[:, b * band : (b + 1) * band].astype(jnp.bfloat16)


def analysis_kernel(half_lats, coeff_ref, table_ref, out_ref):
    bands, group, count, band = coeff_ref.shape
    lanes = 2 * HALF
    flip = reversal(lanes, half_lats)
    parity = lax.broadcasted_iota(jnp.int32, out_ref.shape[1:], 1) % 2
    fill = jnp.zeros((count, lanes - half_lats), jnp.float32)
    for m in range(group):
        bits = [coeff_ref[b, m].astype(jnp.float32) for b in range(bands)]
        north = jnp.concatenate(bits[: bands // 2] + [fill], axis=1)
        south = jnp.concatenate(bits[bands // 2 :] + [fill], axis=1).astype(jnp.bfloat16)
        south = jnp.dot(south, flip, preferred_element_type=jnp.float32)
        if m % 2:
            south = -south
        both = jnp.concatenate([north + south, north - south], axis=0).astype(jnp.bfloat16)
        sums = lax.dot_general(
            both, table_ref[m], (((1,), (1,)), ((), ())), preferred_element_type=jnp.float32
        )
        out_ref[m] = jnp.where(parity == 0, sums[:count], sums[count:])


def synthesis(spectral, orders, lat_total, bands):
    parts, levels, waves, degrees = spectral.shape
    half_lats = lat_total // 2
    count = parts * levels
    lanes = 2 * HALF
    fa, fb, log_start, sin_lat, valid = recurrence_inputs(orders, lat_total, degrees)
    order = jnp.broadcast_to(orders[:, None], (waves, lanes))
    coeffs = jnp.transpose(spectral.astype(jnp.bfloat16), (2, 0, 1, 3)).reshape(
        waves, count, degrees
    )
    band = lat_total // bands
    factor_spec = pl.BlockSpec((degrees // CHUNK, GROUP, CHUNK), lambda g: (0, g, 0))
    wide_spec = pl.BlockSpec((GROUP, lanes), lambda g: (g, 0))
    row_spec = pl.BlockSpec((1, lanes), lambda g: (0, 0))
    return pl.pallas_call(
        functools.partial(synthesis_kernel, half_lats),
        grid=(waves // GROUP,),
        in_specs=[
            factor_spec,
            factor_spec,
            wide_spec,
            row_spec,
            row_spec,
            wide_spec,
            pl.BlockSpec((GROUP, count, degrees), lambda g: (g, 0, 0)),
        ],
        out_specs=[
            pl.BlockSpec((GROUP, degrees, lanes), lambda g: (g, 0, 0)),
            pl.BlockSpec((bands, GROUP, count, band), lambda g: (0, g, 0, 0)),
        ],
        out_shape=[
            jax.ShapeDtypeStruct((waves, degrees, lanes), jnp.bfloat16),
            jax.ShapeDtypeStruct((bands, waves, count, band), jnp.bfloat16),
        ],
        scratch_shapes=[pltpu.VMEM((2, degrees * GROUP, HALF), jnp.float32)],
        compiler_params=pltpu.CompilerParams(vmem_limit_bytes=40 << 20),
    )(fa, fb, log_start, sin_lat, valid, order, coeffs)


def analysis(coeffs, table, lat_total):
    bands, waves, count, band = coeffs.shape
    degrees, lanes = table.shape[1:]
    group = 8
    return pl.pallas_call(
        functools.partial(analysis_kernel, lat_total // 2),
        grid=(waves // group,),
        in_specs=[
            pl.BlockSpec((bands, group, count, band), lambda g: (0, g, 0, 0)),
            pl.BlockSpec((group, degrees, lanes), lambda g: (g, 0, 0)),
        ],
        out_specs=pl.BlockSpec((group, count, degrees), lambda g: (g, 0, 0)),
        out_shape=jax.ShapeDtypeStruct((waves, count, degrees), jnp.float32),
        compiler_params=pltpu.CompilerParams(vmem_limit_bytes=40 << 20),
    )(coeffs, table)


def pick_kernel(index_ref, shift_ref, count_ref, grid_ref, out_ref):
    target = pl.program_id(0)
    levels, capacity = out_ref.shape[1:]
    out_ref[...] = jnp.zeros(out_ref.shape, out_ref.dtype)
    lane = lax.broadcasted_iota(jnp.int32, (levels, HALF), 1)

    def block(b, carry):
        base = b * HALF
        total = jnp.zeros((levels, HALF), jnp.float32)
        for q in range(HALF):
            at = target * capacity + base + q
            moved = pltpu.roll(grid_ref[index_ref[at]], shift_ref[at], 1)
            total = jnp.where(lane == q, moved, total)
        out_ref[0, :, pl.ds(pl.multiple_of(base, HALF), HALF)] = total.astype(out_ref.dtype)
        return carry

    lax.fori_loop(0, (count_ref[target] + HALF - 1) // HALF, block, 0)


def pick(index, shift, counts, grid, capacity):
    owners = counts.shape[0]
    levels = grid.shape[1]
    return pl.pallas_call(
        pick_kernel,
        grid_spec=pltpu.PrefetchScalarGridSpec(
            num_scalar_prefetch=3,
            grid=(owners,),
            in_specs=[pl.BlockSpec(grid.shape, lambda t, *_: (0, 0, 0))],
            out_specs=pl.BlockSpec((1, levels, capacity), lambda t, *_: (t, 0, 0)),
        ),
        out_shape=jax.ShapeDtypeStruct((owners, levels, capacity), jnp.bfloat16),
        compiler_params=pltpu.CompilerParams(vmem_limit_bytes=32 << 20),
    )(index, shift, counts, grid)


def spread_kernel(row_ref, lane_ref, count_ref, values_ref, out_ref, *sums):
    owners, levels, capacity = values_ref.shape
    lane = lax.broadcasted_iota(jnp.int32, (levels, HALF), 1)
    most = count_ref[0]
    for o in range(owners):
        sums[o][...] = jnp.zeros(sums[o].shape, jnp.float32)
        most = jnp.maximum(most, count_ref[o])

    def several(group, carry):
        terms = []
        for k in range(4):
            slot = group * 4 + k
            base = pl.multiple_of((slot // HALF) * HALF, HALF)
            spot = slot % HALF
            for o in range(owners):
                to = lane_ref[o * capacity + slot]
                values = values_ref[o, :, pl.ds(base, HALF)]
                moved = pltpu.roll(values, (to - spot) & (HALF - 1), 1)
                terms.append(jnp.where(lane == to, moved, 0.0))
        for k in range(4):
            rows = [row_ref[o * capacity + group * 4 + k] for o in range(owners)]
            added = [sums[o][rows[o]] + terms[k * owners + o] for o in range(owners)]
            for o in range(owners):
                sums[o][rows[o]] = added[o]
        return carry

    lax.fori_loop(0, (most + 3) // 4, several, 0)
    for o in range(owners):
        out_ref[o] = sums[o][...].astype(out_ref.dtype)


def spread(rows, lanes, counts, values, band_rows):
    owners, levels, capacity = values.shape
    shape = (owners, band_rows, levels, HALF)
    return pl.pallas_call(
        spread_kernel,
        grid_spec=pltpu.PrefetchScalarGridSpec(
            num_scalar_prefetch=3,
            grid=(1,),
            in_specs=[pl.BlockSpec(values.shape, lambda g, *_: (0, 0, 0))],
            out_specs=pl.BlockSpec(shape, lambda g, *_: (0, 0, 0, 0)),
            scratch_shapes=[pltpu.VMEM(shape[1:], jnp.float32) for _ in range(owners)],
        ),
        out_shape=jax.ShapeDtypeStruct(shape, jnp.bfloat16),
        compiler_params=pltpu.CompilerParams(vmem_limit_bytes=40 << 20),
    )(rows, lanes, counts, values)


def wave_table(wave_total, lon_total):
    wave_ids = jnp.arange(wave_total, dtype=jnp.int32)
    lon_ids = jnp.arange(lon_total, dtype=jnp.int32)
    phase = (wave_ids[:, None] * lon_ids[None, :] % lon_total).astype(jnp.float32) * (
        2.0 * math.pi / lon_total
    )
    weights = jnp.where(wave_ids == 0, 1.0, 2.0).astype(jnp.float32) / wave_total
    return jnp.stack([weights[:, None] * jnp.cos(phase), -weights[:, None] * jnp.sin(phase)])


def silu_slope(inputs):
    sigmoid_v = jax.nn.sigmoid(inputs)
    return sigmoid_v * (1.0 + inputs * (1.0 - sigmoid_v))


def radiance_pass(
    profiles, observed, pair_counts, usable, channel_weight, weight_in, weight_mid, weight_out
):
    pre_first = jnp.dot(profiles, weight_in, preferred_element_type=jnp.float32)
    act_first = jax.nn.silu(pre_first).astype(jnp.bfloat16)
    pre_second = jnp.dot(act_first, weight_mid, preferred_element_type=jnp.float32)
    act_second = jax.nn.silu(pre_second).astype(jnp.bfloat16)
    evolved = jnp.dot(act_second, weight_out, preferred_element_type=jnp.float32)
    channel_ids = jnp.arange(weight_out.shape[1], dtype=jnp.float32)
    active = (channel_ids[None, :] < 2.0 * pair_counts[:, None]) & usable[:, None]
    misfit = jnp.where(
        active, channel_weight[None, :] * (evolved - observed.astype(jnp.float32)), 0.0
    ).astype(jnp.bfloat16)
    back_second = (
        jnp.dot(misfit, weight_out.T, preferred_element_type=jnp.float32) * silu_slope(pre_second)
    ).astype(jnp.bfloat16)
    back_first = (
        jnp.dot(back_second, weight_mid.T, preferred_element_type=jnp.float32)
        * silu_slope(pre_first)
    ).astype(jnp.bfloat16)
    return jnp.dot(back_first, weight_in.T, preferred_element_type=jnp.float32).astype(jnp.bfloat16)


def per_device(
    spectral,
    background,
    columns,
    counts,
    radiances,
    used_pairs,
    channel_weight,
    weight_in,
    weight_mid,
    weight_out,
):
    lat_index = lax.axis_index("lat")
    parts, levels, waves_local, degrees = spectral.shape
    bands = M // waves_local
    orders = lat_index * waves_local + jnp.arange(waves_local, dtype=jnp.int32)
    table, fourier = synthesis(spectral, orders, NLAT, bands)
    fourier = lax.all_to_all(fourier, "lat", split_axis=0, concat_axis=0, tiled=True)
    band = fourier.shape[3]
    fourier = fourier.reshape(M, parts, levels, band)
    dft_table = wave_table(M, NLON).astype(jnp.bfloat16)
    band_rows, tile_cols, all_levels = background.shape
    local_cols = columns[0]
    owners = all_levels // levels
    capacity = local_cols.shape[0]
    listed = jnp.concatenate([local_cols, jnp.broadcast_to(counts, (HALF,))])
    listed = lax.all_gather(listed, "lev")
    band_counts = listed[:, capacity]
    listed = listed[:, :capacity]
    tiles = NLON // HALF
    list_rows = listed // tile_cols
    list_lanes = listed % tile_cols
    list_lons = list_lanes + jnp.arange(owners, dtype=jnp.int32)[:, None] * tile_cols
    spots = jnp.arange(capacity, dtype=jnp.int32) % HALF
    index = (list_rows * tiles + list_lons // HALF).reshape(-1)
    shift = ((spots[None, :] - list_lons) % HALF).reshape(-1)
    increment = jnp.einsum(
        "mclj,cmtx->jtlx",
        fourier,
        dft_table.reshape(parts, M, tiles, HALF),
        preferred_element_type=jnp.float32,
    ).reshape(band * tiles, levels, HALF)
    picked = pick(index, shift, band_counts, increment, capacity)
    picked = lax.all_to_all(picked, "lev", split_axis=0, concat_axis=0, tiled=True)
    picked = picked.reshape(all_levels, capacity)
    cell_rows = background.reshape(band_rows * tile_cols, all_levels)
    own_rows = jnp.take(cell_rows, local_cols, axis=0).astype(jnp.float32)
    profiles = (own_rows + picked.T.astype(jnp.float32)).astype(jnp.bfloat16)
    usable = jnp.arange(capacity, dtype=jnp.int32) < counts[0]
    observed = radiances[0]
    pair_counts = used_pairs[0].astype(jnp.float32)
    block_grad = radiance_pass(
        profiles, observed, pair_counts, usable, channel_weight, weight_in, weight_mid, weight_out
    )
    grid_grad = (
        jnp.zeros(cell_rows.shape, jnp.float32).at[local_cols].add(block_grad.astype(jnp.float32))
    )
    grid_grad = grid_grad.reshape(band_rows, tile_cols, all_levels)
    sent = block_grad.T.reshape(owners, levels, capacity)
    sent = lax.all_to_all(sent, "lev", split_axis=0, concat_axis=0, tiled=True)
    grad_rows = spread(
        list_rows.reshape(-1),
        list_lanes.reshape(-1),
        band_counts,
        sent.astype(jnp.float32),
        band_rows,
    )
    tile_table = dft_table.reshape(parts, M, owners, tile_cols)
    tile_table = jnp.pad(tile_table, ((0, 0), (0, 0), (0, 0), (0, HALF - tile_cols)))
    coeff_grad = jnp.einsum(
        "ojlx,cmox->mclj", grad_rows, tile_table, preferred_element_type=jnp.float32
    ).astype(jnp.bfloat16)
    coeff_grad = coeff_grad.reshape(bands, waves_local, parts * levels, band)
    coeff_grad = lax.all_to_all(coeff_grad, "lat", split_axis=0, concat_axis=0, tiled=True)
    spectral_grad = analysis(coeff_grad, table, NLAT)
    spectral_grad = jnp.transpose(
        spectral_grad.reshape(waves_local, parts, levels, degrees), (1, 2, 0, 3)
    )
    return (spectral_grad, grid_grad)


def solution(mesh):
    in_specs = (
        P(None, "lev", "lat", None),
        P("lat", "lev", None),
        P(("lat", "lev"), None),
        P(("lat", "lev")),
        P(("lat", "lev"), None, None),
        P(("lat", "lev"), None),
        P(),
        P(),
        P(),
        P(),
    )
    out_specs = (P(None, "lev", "lat", None), P("lat", "lev", None))
    return jax.shard_map(
        per_device, mesh=mesh, in_specs=in_specs, out_specs=out_specs, check_vma=False
    )
```
